768 devices in a mesh: section: 8 (over y), expert: 24 (over x_lo, z), dp: 4 (over x_hi, core).
Axes of the slice: x: 4 (x_hi: 2, x_lo: 2; x = x_hi * 2 + x_lo), y: 8, z: 12, core: 2. Of those that a mesh axis runs over, the one named last changes fastest.
Arguments:
- tokens_fwd: bfloat16 [8, 3072, 7168], P('section', 'expert', 'dp'), may hold values from -6 to 6
- routes_fwd: int32 [8, 3072, 1], P('section', 'expert'), may hold values from 0 to 5; in each aligned block of 128 rows (0 to 127, 128 to 255, ..., all dimensions but the last counted through in order) at most 22 rows name the same one
- gates_fwd: float32 [8, 3072, 1], P('section', 'expert'), may hold values from 0.2 to 1
- cotangent: bfloat16 [8, 3072, 7168], P('section', 'expert', 'dp'), may hold values from -6 to 6
- routes_bwd: int32 [8, 3072, 1], P('section', 'expert'), may hold values from 0 to 5; in each aligned block of 128 rows (0 to 127, 128 to 255, ..., all dimensions but the last counted through in order) at most 22 rows name the same one
- gates_bwd: float32 [8, 3072, 1], P('section', 'expert'), may hold values from 0.2 to 1
- saved_pre: bfloat16 [8, 528, 2, 6144], P('section', None, None, 'expert'), may hold values from -6 to 6
- w_gate: bfloat16 [8, 7168, 6144], P('section', 'dp', 'expert'), may hold values from -0.0625 to 0.0625
- w_up: bfloat16 [8, 7168, 6144], P('section', 'dp', 'expert'), may hold values from -0.0625 to 0.0625
- w_down: bfloat16 [8, 6144, 7168], P('section', 'expert', 'dp'), may hold values from -0.1875 to 0.1875
Outputs:
- forwarded: bfloat16 [8, 3072, 7168], P('section', 'expert', 'dp')
- returned: bfloat16 [8, 3072, 7168], P('section', 'expert', 'dp')
The draws below stay inside these ranges and needn't reach their ends.
Inputs may be any that keep to these rules, and one draw needn't show every extreme that they name: `routes_fwd`: each token names 1 different experts; in each aligned block of 128 tokens (the tokens of one index of expert) no expert is named more than 22 times. `routes_bwd`: each token names 1 different experts; in each aligned block of 128 tokens (the tokens of one index of expert) no expert is named more than 22 times.
All inputs are finite; a program needn't handle non-finite values.
Results may differ from the reference program's by a relative error of at most 0.0065.
Values may be sent and summed in bfloat16 or wider, within the bound.
No kernel may reach another device: no remote copies, remote signals or barrier semaphores. Data moves between devices by JAX's collectives and lax.ppermute only.
A program may use at most 32 MiB of HBM per device.

```python
import math
import jax
import jax.numpy as jnp
import numpy as np
from jax import lax

D = 7168
HID = 1024
GROUP = 4
TOP = 1
ROWS = 128
SECTIONS = 8
EXPERTS = 6
CAP = 22
TOKENS = 3072
SLOTS = 528
N_EXPERT = 24


def level_of(rng, shape, shards, least, top_value):
    def one(dim, shards_of):
        heights = jax.random.uniform(jax.random.fold_in(jax.random.fold_in(rng, 6), dim), (shards_of,), jnp.float32, least / len(shards), top_value / len(shards))
        return jnp.repeat(jnp.exp(heights), shape[dim] // shards_of).reshape((-1,) + (1,) * (len(shape) - dim - 1))

    factor_of = one(*shards[0])
    for cut in shards[1:]:
        factor_of = factor_of * one(*cut)
    return factor_of


def shared_out(own_key, own, number, rows, count, top, most, skew):
    sequence = jax.random.permutation(own_key, count)
    packed, common = shares(count, rows * top, most, skew, True), shares(count, rows * top, most, skew, False)
    places = jnp.arange(count)

    def named(lengths, offset_by):
        used = int((lengths > 0).sum())
        fixed = max(1, used // 4)
        moved = fixed + (places - fixed + offset_by * (used - fixed)) % max(1, count - fixed)
        return jnp.zeros((count,), jnp.int32).at[sequence[jnp.where(places < fixed, places, moved)]].set(jnp.asarray(lengths, jnp.int32))

    lengths = jnp.where(number % 4 == 0, named(packed, number // 4), named(common, number - number // 4 - 1))
    mixed = jax.random.permutation(jax.random.fold_in(own, 3), count)
    source_of, sink = mixed[0:count // 2 * 2:2], mixed[1:count // 2 * 2:2]
    slack = jnp.minimum(lengths[source_of] - 1, most - lengths[sink]) // 2
    slack = jnp.where((source_of == sequence[0]) | (sink == sequence[0]) | (lengths[sink] == 0), 0, jnp.maximum(slack, 0))
    moved = jax.random.randint(jax.random.fold_in(own, 4), (count // 2,), 0, 1 << 20) % (slack + 1)
    lengths = lengths.at[source_of].add(-moved).at[sink].add(moved)
    items = jnp.searchsorted(jnp.cumsum(lengths), jnp.arange(rows * top), side="right").astype(jnp.int32)
    grid = items.reshape(top, rows).T
    grid = grid[jax.random.permutation(jax.random.fold_in(own, 1), rows)]
    offset_by = jax.random.randint(jax.random.fold_in(own, 2), (rows, 1), 0, top)
    return jnp.take_along_axis(grid, (jnp.arange(top)[None, :] + offset_by) % top, axis=1)


def shares(count, total, limit, lean, full):
    loads = [(1 << 20) // math.isqrt(rank ** lean) + 1 for rank in range(1, count + 1)]
    largest = limit if full else min(limit, max(-(-total // count), total * loads[0] // sum(loads)))
    least = 1 if total - largest >= count - 1 else 0
    given, spare = [largest] + [least] * (count - 1), total - largest - least * (count - 1)
    while spare > 0:
        free = [i for i in range(1, count) if given[i] < largest] or [i for i in range(1, count) if given[i] < limit]
        pool, remaining = sum([loads[i] for i in free]), spare
        for i in free:
            addition = min(limit - given[i], max(1, remaining * loads[i] // pool), spare)
            given[i] = given[i] + addition
            spare = spare - addition
    return np.array(given)


def centred(rng, dims, spread, bound, cuts=(), held_as=jnp.bfloat16):
    gain = level_of(rng, dims, cuts, -0.22, 0.18) if cuts else 1.0
    result = jax.random.normal(rng, dims, jnp.float32) * spread * gain
    return jnp.minimum(jnp.maximum(result, -bound), bound).astype(held_as)


def setup_inputs(seed: int = 0) -> dict:
    key_of = jax.random.split(jax.random.key(seed), 11)
    tokens_fwd = centred(key_of[0], (SECTIONS, TOKENS, D), 1.0, 6.0, ((0, 8), (1, 24), (2, 4)))
    routes_fwd_keys = jax.random.split(jax.random.fold_in(key_of[1], 1), SECTIONS * TOKENS // ROWS)
    routes_fwd_turns = jax.random.permutation(jax.random.fold_in(key_of[1], 3), SECTIONS * TOKENS // ROWS)
    routes_fwd = jax.vmap(lambda own, number: shared_out(jax.random.fold_in(key_of[1], 2), own, number, ROWS, EXPERTS, TOP, CAP, 2))(routes_fwd_keys, routes_fwd_turns).reshape((SECTIONS, TOKENS, TOP))
    gates_fwd = jnp.clip(0.2 + 0.8 * jax.random.uniform(key_of[2], (SECTIONS, TOKENS, TOP), jnp.float32) ** level_of(key_of[2], (SECTIONS, TOKENS, TOP), ((0, 8), (1, 24)), -0.2, 0.2), 0.2, 1.0)
    cotangent = centred(key_of[3], (SECTIONS, TOKENS, D), 1.0, 6.0, ((0, 8), (1, 24), (2, 4)))
    routes_bwd_keys = jax.random.split(jax.random.fold_in(key_of[4], 1), SECTIONS * TOKENS // ROWS)
    routes_bwd_turns = jax.random.permutation(jax.random.fold_in(key_of[4], 3), SECTIONS * TOKENS // ROWS)
    routes_bwd = jax.vmap(lambda own, number: shared_out(jax.random.fold_in(key_of[4], 2), own, number, ROWS, EXPERTS, TOP, CAP, 2))(routes_bwd_keys, routes_bwd_turns).reshape((SECTIONS, TOKENS, TOP))
    gates_bwd = jnp.clip(0.2 + 0.8 * jax.random.uniform(key_of[5], (SECTIONS, TOKENS, TOP), jnp.float32) ** level_of(key_of[5], (SECTIONS, TOKENS, TOP), ((0, 8), (1, 24)), -0.2, 0.2), 0.2, 1.0)
    saved_pre = centred(key_of[6], (SECTIONS, SLOTS, 2, EXPERTS * HID), 1.0, 6.0, ((0, 8), (3, 24)))
    w_gate = centred(key_of[7], (SECTIONS, D, EXPERTS * HID), D ** -0.5, 0.0625, ((0, 8), (1, 4), (2, 24)))
    w_up = centred(key_of[8], (SECTIONS, D, EXPERTS * HID), D ** -0.5, 0.0625, ((0, 8), (1, 4), (2, 24)))
    w_down = centred(key_of[9], (SECTIONS, EXPERTS * HID, D), HID ** -0.5, 0.1875, ((0, 8), (1, 24), (2, 4)))
    return {"tokens_fwd": tokens_fwd, "routes_fwd": routes_fwd, "gates_fwd": gates_fwd, "cotangent": cotangent, "routes_bwd": routes_bwd, "gates_bwd": gates_bwd, "saved_pre": saved_pre, "w_gate": w_gate, "w_up": w_up, "w_down": w_down}


def silu_plain(values):
    return values * jax.nn.sigmoid(values)


def route_tables(routes, gate_values):
    expert_ids = jnp.arange(EXPERTS, dtype=jnp.int32)
    matches = routes[:, :, None] == expert_ids[None, None, :]
    member = jnp.sum(matches.astype(jnp.int32), axis=1)
    weighting = jnp.sum(jnp.where(matches, gate_values[:, :, None], jnp.zeros_like(gate_values[:, :, None])), axis=1)
    member = member.reshape(N_EXPERT, ROWS, EXPERTS).transpose(0, 2, 1)
    weighting = weighting.reshape(N_EXPERT, ROWS, EXPERTS).transpose(0, 2, 1)
    before = jnp.cumsum(member, axis=2) - member
    slot_ids = jnp.arange(CAP, dtype=jnp.int32)
    hit = (before[:, :, None, :] == slot_ids[None, None, :, None]).astype(jnp.int32)
    placing = (member[:, :, None, :] * hit).astype(jnp.float32)
    return placing, weighting


def fill_slots(placing, values):
    blocks = values.reshape(N_EXPERT, ROWS, D)
    filled = jnp.einsum('iecr,ird->eicd', placing, blocks, precision=lax.Precision.HIGHEST)
    return filled.reshape(EXPERTS, N_EXPERT * CAP, D).astype(jnp.bfloat16)


def gather_rows(placing, per_slot):
    shaped = per_slot.reshape(EXPERTS, N_EXPERT, CAP, D)
    rows_out = jnp.einsum('iecr,eicd->ird', placing, shaped, precision=lax.Precision.HIGHEST)
    return rows_out.reshape(N_EXPERT * ROWS, D)


def rounded_sum(pieces):
    narrow = lax.optimization_barrier(pieces.astype(jnp.bfloat16))
    return jnp.sum(narrow.astype(jnp.float32), axis=0)


def reference(tokens_fwd, routes_fwd, gates_fwd, cotangent, routes_bwd, gates_bwd, saved_pre, w_gate, w_up, w_down):
    piece_width = HID // GROUP
    slot_total = N_EXPERT * CAP
    outputs = []
    gradients = []
    for section_id in range(SECTIONS):
        placing, weighting = route_tables(routes_fwd[section_id], gates_fwd[section_id])
        slots_in = fill_slots(placing, tokens_fwd[section_id].astype(jnp.float32))
        placing_grad, weighting_grad = route_tables(routes_bwd[section_id], gates_bwd[section_id])
        slots_grad = fill_slots(placing_grad * weighting_grad[:, :, None, :], cotangent[section_id].astype(jnp.float32))
        summed_out = []
        summed_grad = []
        for expert_id in range(EXPERTS):
            low_col = expert_id * HID
            high_col = low_col + HID
            gate_pre = jnp.dot(slots_in[expert_id], w_gate[section_id][:, low_col:high_col], preferred_element_type=jnp.float32)
            up_pre = jnp.dot(slots_in[expert_id], w_up[section_id][:, low_col:high_col], preferred_element_type=jnp.float32)
            hidden = (silu_plain(gate_pre) * up_pre).astype(jnp.bfloat16)
            down_block = w_down[section_id][low_col:high_col].reshape(GROUP, piece_width, D).astype(jnp.float32)
            pieces = jnp.einsum('sgh,ghd->gsd', hidden.reshape(slot_total, GROUP, piece_width).astype(jnp.float32), down_block)
            summed_out.append(rounded_sum(pieces))
            grad_hidden = lax.dot_general(slots_grad[expert_id], w_down[section_id][low_col:high_col], (((1,), (1,)), ((), ())), preferred_element_type=jnp.float32)
            pre_gate = saved_pre[section_id][:, 0, low_col:high_col].astype(jnp.float32)
            pre_up = saved_pre[section_id][:, 1, low_col:high_col].astype(jnp.float32)
            sigmoid_gate = jax.nn.sigmoid(pre_gate)
            grad_gate = (grad_hidden * pre_up * sigmoid_gate * (1.0 + pre_gate * (1.0 - sigmoid_gate))).astype(jnp.bfloat16)
            grad_up = (grad_hidden * pre_gate * sigmoid_gate).astype(jnp.bfloat16)
            gate_block = w_gate[section_id][:, low_col:high_col].reshape(D, GROUP, piece_width).astype(jnp.float32)
            up_block = w_up[section_id][:, low_col:high_col].reshape(D, GROUP, piece_width).astype(jnp.float32)
            grad_pieces = jnp.einsum('sgh,dgh->gsd', grad_gate.reshape(slot_total, GROUP, piece_width).astype(jnp.float32), gate_block)
            grad_pieces = grad_pieces + jnp.einsum('sgh,dgh->gsd', grad_up.reshape(slot_total, GROUP, piece_width).astype(jnp.float32), up_block)
            summed_grad.append(rounded_sum(grad_pieces))
        scaled = placing * weighting[:, :, None, :]
        outputs.append(gather_rows(scaled, jnp.stack(summed_out)).astype(jnp.bfloat16))
        gradients.append(gather_rows(placing_grad, jnp.stack(summed_grad)).astype(jnp.bfloat16))
    layer_out = jnp.stack(outputs)
    layer_grad = jnp.stack(gradients)
    zero_section = jnp.zeros_like(layer_out[:1])
    forwarded = jnp.concatenate([zero_section, layer_out[:-1]], axis=0)
    returned = jnp.concatenate([layer_grad[1:], zero_section], axis=0)
    return forwarded, returned
```

```python
import jax
import jax.numpy as jnp
from jax import lax
from jax.sharding import Mesh
from jax.sharding import PartitionSpec as P

GROUP = 4
PAD = 8
RING = ("group", "member")
BF16 = jnp.bfloat16
F32 = jnp.float32


def hop(values, step):
    count = lax.axis_size(RING)
    return lax.ppermute(values, RING, [(i, (i + step) % count) for i in range(count)])


def swap(values, axis):
    return lax.ppermute(values, axis, [(0, 1), (1, 0)])


def placing_of(routes, capacity, width):
    groups = lax.axis_size("group")
    half, group = lax.axis_index("half"), lax.axis_index("group")
    near = [half * groups + (group + k) % groups for k in range(groups)]
    far = [(1 - half) * groups + (group + k) % groups for k in range(groups)]
    ids = jnp.stack(near + far).astype(jnp.int32)
    member = (routes[None, :, 0] == ids[:, None]).astype(jnp.int32)
    before = jnp.cumsum(member, axis=1) - member
    slot_ids = jnp.arange(width, dtype=jnp.int32)
    hit = (before[:, None, :] == slot_ids[None, :, None]) & (slot_ids < capacity)[None, :, None]
    placing = jnp.where(hit & (member[:, None, :] > 0), 1.0, 0.0).astype(BF16)
    return placing.reshape(-1, routes.shape[0])


def dispatch(slots):
    member = lax.axis_index("member")
    other = swap(slots[1], "half")
    blocks = jnp.concatenate([slots[0], other], axis=1)
    own = blocks[0]
    right = jnp.stack([blocks[0], blocks[1]])
    left = jnp.stack([blocks[0], blocks[2]])
    rights, lefts = {}, {}
    for step in range(1, 8):
        if step == 4:
            right, left = right[1], left[1]
        right, left = hop(right, 1), hop(left, -1)
        rights[step], lefts[step] = right, left
    out = [jnp.stack([own, lefts[4], rights[4]])]
    for s in range(1, GROUP):
        out.append(
            jnp.stack(
                [
                    jnp.where(member >= s, rights[s][0], lefts[4 - s][0]),
                    jnp.where(member >= s, lefts[4 - s][1], lefts[8 - s]),
                    jnp.where(member < s, rights[s][1], rights[s + 4]),
                ]
            )
        )
    return jnp.stack(out)


def collect(parts):
    member = lax.axis_index("member")
    width = parts.shape[2] // 2
    zero = jnp.zeros_like(parts[0, 0])

    def only(mask, values):
        return jnp.where(mask, values, zero)

    right = only(member >= 3, parts[3, 2])
    left = only(member < 1, parts[1, 1])
    for s in (2, 1):
        right = hop(right, -1) + only(member >= s, parts[s, 2])
        left = hop(left, 1) + only(member < 4 - s, parts[4 - s, 1])
    right = hop(right, -1) + parts[0, 2]
    left = hop(left, 1) + parts[0, 1]
    right = jnp.stack([only(member >= 3, parts[3, 0]), hop(right, -1) + only(member < 3, parts[3, 2])])
    left = jnp.stack([only(member < 1, parts[1, 0]), hop(left, 1) + only(member >= 1, parts[1, 1])])
    for s in (2, 1):
        right = hop(right, -1) + jnp.stack(
            [only(member >= s, parts[s, 0]), only(member < s, parts[s, 2])]
        )
        left = hop(left, 1) + jnp.stack(
            [only(member < 4 - s, parts[4 - s, 0]), only(member >= 4 - s, parts[4 - s, 1])]
        )
    right = hop(right, -1)
    left = hop(left, 1)
    blocks = jnp.stack([parts[0, 0] + right[0] + left[0], right[1], left[1]])
    mine, others = blocks[:, :width], blocks[:, width:]
    return jnp.stack([mine, swap(others, "half")])


def halves(values, axis):
    place = lax.axis_index(axis)
    half = values.shape[0] // 2
    low, high = values[:half], values[half:]
    return jnp.where(place == 0, low, high), jnp.where(place == 0, high, low)


def reduce_rows(values):
    for axis in ("core", "far"):
        kept, sent = halves(values, axis)
        values = kept + swap(sent.astype(BF16), axis).astype(F32)
    return values


def gather_rows(values):
    for axis in ("far", "core"):
        place = lax.axis_index(axis)
        other = swap(values, axis)
        values = jnp.concatenate(
            [jnp.where(place == 0, values, other), jnp.where(place == 0, other, values)]
        )
    return values


def contract_last(left_side, right_side):
    return lax.dot_general(
        left_side, right_side, (((1,), (1,)), ((), ())), preferred_element_type=F32
    )


def saved_quarter(saved, capacity, width):
    groups = lax.axis_size("group")
    half, group, member = (lax.axis_index(name) for name in ("half", "group", "member"))
    quarter = lax.axis_index("core") * 2 + lax.axis_index("far")
    source = (member - quarter) % GROUP
    blocks = saved.reshape(2, groups, GROUP, capacity, *saved.shape[1:])
    blocks = lax.dynamic_index_in_dim(blocks, source, axis=2, keepdims=False)
    rolled = [
        lax.dynamic_index_in_dim(blocks, (group + k) % groups, axis=1, keepdims=False)
        for k in range(groups)
    ]
    out = jnp.stack(rolled)
    out = jnp.where(half == 0, out, out[:, ::-1])
    out = jnp.pad(out, ((0, 0), (0, 0), (0, width - capacity), (0, 0), (0, 0)))
    return out.reshape(groups * 2 * width, *saved.shape[1:])


def shards(
    tokens_fwd,
    routes_fwd,
    gates_fwd,
    cotangent,
    routes_bwd,
    gates_bwd,
    saved_pre,
    w_gate,
    w_up,
    w_down,
):
    groups = lax.axis_size("group")
    devices = 2 * groups * GROUP
    capacity = saved_pre.shape[1] // devices
    width = -(-capacity // PAD) * PAD
    columns = tokens_fwd.shape[2]

    place_fwd = placing_of(routes_fwd[0], capacity, width)
    place_bwd = placing_of(routes_bwd[0], capacity, width)
    send_fwd = jnp.dot(place_fwd, tokens_fwd[0], preferred_element_type=F32).astype(BF16)
    scaled = (cotangent[0].astype(F32) * gates_bwd[0]).astype(BF16)
    send_bwd = jnp.dot(place_bwd, scaled, preferred_element_type=F32).astype(BF16)

    got_fwd = dispatch(send_fwd.reshape(2, groups, width, columns)).reshape(-1, columns)
    part = jnp.concatenate(
        [
            jnp.dot(got_fwd, w_gate[0], preferred_element_type=F32),
            jnp.dot(got_fwd, w_up[0], preferred_element_type=F32),
        ],
        axis=1,
    )
    got_bwd = dispatch(send_bwd.reshape(2, groups, width, columns)).reshape(-1, columns)
    summed = reduce_rows(part)
    hidden_width = w_gate.shape[2]
    gate_pre, up_pre = summed[:, :hidden_width], summed[:, hidden_width:]
    hidden = gather_rows((gate_pre * jax.nn.sigmoid(gate_pre) * up_pre).astype(BF16))
    out = jnp.dot(hidden, w_down[0], preferred_element_type=F32).astype(BF16)
    back_fwd = collect(out.reshape(GROUP, groups, 2 * width, columns)).reshape(-1, columns)

    grad_hidden = reduce_rows(contract_last(got_bwd, w_down[0]))
    saved = saved_quarter(saved_pre[0], capacity, width)
    pre_gate = saved[:, 0].astype(F32)
    pre_up = saved[:, 1].astype(F32)
    sigmoid_gate = jax.nn.sigmoid(pre_gate)
    grad_gate = grad_hidden * pre_up * sigmoid_gate * (1.0 + pre_gate * (1.0 - sigmoid_gate))
    grad_up = grad_hidden * pre_gate * sigmoid_gate
    grads = gather_rows(jnp.concatenate([grad_gate, grad_up], axis=1).astype(BF16))
    grad_out = (
        contract_last(grads[:, :hidden_width], w_gate[0])
        + contract_last(grads[:, hidden_width:], w_up[0])
    ).astype(BF16)
    back_bwd = collect(grad_out.reshape(GROUP, groups, 2 * width, columns)).reshape(-1, columns)

    def rows_of(placing, values):
        return lax.dot_general(
            placing, values, (((0,), (0,)), ((), ())), preferred_element_type=F32
        )

    layer_out = (rows_of(place_fwd, back_fwd) * gates_fwd[0]).astype(BF16)
    layer_grad = rows_of(place_bwd, back_bwd).astype(BF16)
    ends = lax.axis_size("section") - 1
    forwarded = lax.ppermute(layer_out, "section", [(i, i + 1) for i in range(ends)])
    returned = lax.ppermute(layer_grad, "section", [(i + 1, i) for i in range(ends)])
    return (forwarded[None], returned[None])


def solution(mesh):
    sections, expert_devices, quarters = (mesh.shape[name] for name in ("section", "expert", "dp"))
    fine = Mesh(
        mesh.devices.reshape(sections, 2, expert_devices // 2 // GROUP, GROUP, 2, quarters // 2),
        ("section", "half", "group", "member", "far", "core"),
    )
    expert, dp = ("half", "group", "member"), ("far", "core")
    return jax.shard_map(
        shards,
        mesh=fine,
        in_specs=(
            P("section", expert, dp),
            P("section", expert, None),
            P("section", expert, None),
            P("section", expert, dp),
            P("section", expert, None),
            P("section", expert, None),
            P("section", None, None, expert),
            P("section", dp, expert),
            P("section", dp, expert),
            P("section", expert, dp),
        ),
        out_specs=(P("section", expert, dp), P("section", expert, dp)),
        check_vma=False,
    )
```

```python
import jax
import jax.numpy as jnp
from jax import lax
from jax.sharding import Mesh
from jax.sharding import PartitionSpec as P

GROUP = 4
PAD = 8
RING = ("group", "member")
BF16 = jnp.bfloat16
F32 = jnp.float32


def hop(values, step):
    count = lax.axis_size(RING)
    return lax.ppermute(values, RING, [(i, (i + step) % count) for i in range(count)])


def swap(values, axis):
    return lax.ppermute(values, axis, [(0, 1), (1, 0)])


def placing_of(routes, capacity, width):
    groups = lax.axis_size("group")
    half, group = lax.axis_index("half"), lax.axis_index("group")
    near = [half * groups + (group + k) % groups for k in range(groups)]
    far = [(1 - half) * groups + (group + k) % groups for k in range(groups)]
    ids = jnp.stack(near + far).astype(jnp.int32)
    member = (routes[None, :, 0] == ids[:, None]).astype(jnp.int32)
    before = jnp.cumsum(member, axis=1) - member
    slot_ids = jnp.arange(width, dtype=jnp.int32)
    hit = (before[:, None, :] == slot_ids[None, :, None]) & (slot_ids < capacity)[None, :, None]
    placing = jnp.where(hit & (member[:, None, :] > 0), 1.0, 0.0).astype(BF16)
    return placing.reshape(-1, routes.shape[0])


def around(values, step):
    return lax.ppermute(values, "member", [(i, (i + step) % GROUP) for i in range(GROUP)])


def dispatch(slots, step):
    blocks = jnp.concatenate([slots[0], swap(slots[1], "half")], axis=1)
    part = jnp.stack([blocks[0], hop(blocks[2], -GROUP), hop(blocks[1], GROUP)])
    part = part.reshape(-1, slots.shape[-1])
    parts = [part]
    for _ in range(1, GROUP):
        part = around(part, step)
        parts.append(part)
    return parts


def collect(parts, step, groups):
    total = parts[GROUP - 1]
    for k in range(GROUP - 2, -1, -1):
        total = around(total, -step) + parts[k]
    total = total.reshape(groups, 2, -1, total.shape[-1])
    blocks = jnp.stack([total[0], hop(total[2], -GROUP), hop(total[1], GROUP)])
    return jnp.stack([blocks[:, 0], swap(blocks[:, 1], "half")])


def reduce_rows(parts):
    place = lax.axis_index("core")
    low = jnp.concatenate(parts[: GROUP // 2])
    high = jnp.concatenate(parts[GROUP // 2 :])
    kept, sent = jnp.where(place == 0, low, high), jnp.where(place == 0, high, low)
    kept = kept + swap(sent, "core")
    return kept + swap(kept.astype(BF16), "far").astype(F32)


def gather_rows(values):
    place = lax.axis_index("core")
    other = swap(values, "core")
    low, high = jnp.where(place == 0, values, other), jnp.where(place == 0, other, values)
    rows = values.shape[0] // 2
    return [low[:rows], low[rows:], high[:rows], high[rows:]]


def contract_last(left_side, right_side):
    return lax.dot_general(
        left_side, right_side, (((1,), (1,)), ((), ())), preferred_element_type=F32
    )


def saved_half(saved, capacity, width, step):
    groups = lax.axis_size("group")
    half, group, member, core = (lax.axis_index(n) for n in ("half", "group", "member", "core"))
    blocks = saved.reshape(2, groups, GROUP, capacity, *saved.shape[1:])
    out = []
    for k in range(GROUP // 2):
        source = (member - step * (core * (GROUP // 2) + k)) % GROUP
        own = lax.dynamic_index_in_dim(blocks, source, axis=2, keepdims=False)
        for g in range(groups):
            at = (group + g) % groups
            pair = lax.dynamic_index_in_dim(own, at, axis=1, keepdims=False)
            out.append(jnp.where(half == 0, pair, pair[::-1]))
    out = jnp.pad(jnp.stack(out), ((0, 0), (0, 0), (0, width - capacity), (0, 0), (0, 0)))
    return out.reshape(-1, *saved.shape[1:])


def shards(
    tokens_fwd,
    routes_fwd,
    gates_fwd,
    cotangent,
    routes_bwd,
    gates_bwd,
    saved_pre,
    w_gate,
    w_up,
    w_down,
):
    groups = lax.axis_size("group")
    devices = 2 * groups * GROUP
    capacity = saved_pre.shape[1] // devices
    width = -(-capacity // PAD) * PAD
    columns = tokens_fwd.shape[2]
    hidden_width = w_gate.shape[2]

    place_fwd = placing_of(routes_fwd[0], capacity, width)
    place_bwd = placing_of(routes_bwd[0], capacity, width)
    send_fwd = jnp.dot(place_fwd, tokens_fwd[0], preferred_element_type=F32).astype(BF16)
    scaled = (cotangent[0].astype(F32) * gates_bwd[0]).astype(BF16)
    send_bwd = jnp.dot(place_bwd, scaled, preferred_element_type=F32).astype(BF16)

    got_fwd = dispatch(send_fwd.reshape(2, groups, width, columns), 1)
    got_bwd = dispatch(send_bwd.reshape(2, groups, width, columns), -1)
    partial_fwd = [
        jnp.concatenate(
            [
                jnp.dot(rows, w_gate[0], preferred_element_type=F32),
                jnp.dot(rows, w_up[0], preferred_element_type=F32),
            ],
            axis=1,
        )
        for rows in got_fwd
    ]
    summed = reduce_rows(partial_fwd)
    gate_pre, up_pre = summed[:, :hidden_width], summed[:, hidden_width:]
    hidden = gather_rows((gate_pre * jax.nn.sigmoid(gate_pre) * up_pre).astype(BF16))
    out = [jnp.dot(rows, w_down[0], preferred_element_type=F32).astype(BF16) for rows in hidden]
    back_fwd = collect(out, 1, groups).reshape(-1, columns)

    grad_hidden = reduce_rows([contract_last(rows, w_down[0]) for rows in got_bwd])
    saved = saved_half(saved_pre[0], capacity, width, -1)
    pre_gate = saved[:, 0].astype(F32)
    pre_up = saved[:, 1].astype(F32)
    sigmoid_gate = jax.nn.sigmoid(pre_gate)
    grad_gate = grad_hidden * pre_up * sigmoid_gate * (1.0 + pre_gate * (1.0 - sigmoid_gate))
    grad_up = grad_hidden * pre_gate * sigmoid_gate
    grads = gather_rows(jnp.concatenate([grad_gate, grad_up], axis=1).astype(BF16))
    grad_out = [
        (
            contract_last(rows[:, :hidden_width], w_gate[0])
            + contract_last(rows[:, hidden_width:], w_up[0])
        ).astype(BF16)
        for rows in grads
    ]
    back_bwd = collect(grad_out, -1, groups).reshape(-1, columns)

    def rows_of(placing, values):
        return lax.dot_general(
            placing, values, (((0,), (0,)), ((), ())), preferred_element_type=F32
        )

    layer_out = (rows_of(place_fwd, back_fwd) * gates_fwd[0]).astype(BF16)
    layer_grad = rows_of(place_bwd, back_bwd).astype(BF16)
    ends = lax.axis_size("section") - 1
    forwarded = lax.ppermute(layer_out, "section", [(i, i + 1) for i in range(ends)])
    returned = lax.ppermute(layer_grad, "section", [(i + 1, i) for i in range(ends)])
    return (forwarded[None], returned[None])


def solution(mesh):
    sections, expert_devices, quarters = (mesh.shape[name] for name in ("section", "expert", "dp"))
    fine = Mesh(
        mesh.devices.reshape(sections, 2, expert_devices // 2 // GROUP, GROUP, 2, quarters // 2),
        ("section", "half", "group", "member", "far", "core"),
    )
    expert, dp = ("half", "group", "member"), ("far", "core")
    return jax.shard_map(
        shards,
        mesh=fine,
        in_specs=(
            P("section", expert, dp),
            P("section", expert, None),
            P("section", expert, None),
            P("section", expert, dp),
            P("section", expert, None),
            P("section", expert, None),
            P("section", None, None, expert),
            P("section", dp, expert),
            P("section", dp, expert),
            P("section", expert, dp),
        ),
        out_specs=(P("section", expert, dp), P("section", expert, dp)),
        check_vma=False,
    )
```

```python
import jax
import jax.numpy as jnp
from jax import lax
from jax.sharding import Mesh
from jax.sharding import PartitionSpec as P

GROUP = 4
PAD = 8
RING = ("group", "member")
BF16 = jnp.bfloat16
F32 = jnp.float32


def hop(values, step):
    count = lax.axis_size(RING)
    return lax.ppermute(values, RING, [(i, (i + step) % count) for i in range(count)])


def swap(values, axis):
    return lax.ppermute(values, axis, [(0, 1), (1, 0)])


def placing_of(routes, capacity, width):
    groups = lax.axis_size("group")
    half, group = lax.axis_index("half"), lax.axis_index("group")
    near = [half * groups + (group + k) % groups for k in range(groups)]
    far = [(1 - half) * groups + (group + k) % groups for k in range(groups)]
    ids = jnp.stack(near + far).astype(jnp.int32)
    member = (routes[None, :] == ids[:, None]).astype(jnp.int32)
    before = jnp.cumsum(member, axis=1) - member
    slot_ids = jnp.arange(width, dtype=jnp.int32)
    hit = (before[:, None, :] == slot_ids[None, :, None]) & (slot_ids < capacity)[None, :, None]
    placing = jnp.where(hit & (member[:, None, :] > 0), 1.0, 0.0).astype(BF16)
    return placing.reshape(-1, routes.shape[0])


def around(values, step):
    return lax.ppermute(values, "member", [(i, (i + step) % GROUP) for i in range(GROUP)])


def widen(slots):
    return jnp.concatenate([slots[0], swap(slots[1], "half")], axis=1)


def shift_groups(blocks):
    return blocks[0], hop(blocks[2], -GROUP), hop(blocks[1], GROUP)


def reduce_rows(parts):
    place = lax.axis_index("core")
    low = jnp.concatenate(parts[: GROUP // 2])
    high = jnp.concatenate(parts[GROUP // 2 :])
    kept, sent = jnp.where(place == 0, low, high), jnp.where(place == 0, high, low)
    kept = kept + swap(sent, "core")
    return kept + swap(kept.astype(BF16), "far").astype(F32)


def gather_rows(values):
    place = lax.axis_index("core")
    other = swap(values, "core")
    low, high = jnp.where(place == 0, values, other), jnp.where(place == 0, other, values)
    rows = values.shape[0] // 2
    return [low[:rows], low[rows:], high[:rows], high[rows:]]


def contract_last(left_side, right_side):
    return lax.dot_general(
        left_side, right_side, (((1,), (1,)), ((), ())), preferred_element_type=F32
    )


def saved_half(saved, capacity, width, step):
    groups = lax.axis_size("group")
    half, group, member, core = (lax.axis_index(n) for n in ("half", "group", "member", "core"))
    blocks = saved.reshape(2, groups, GROUP, capacity, *saved.shape[1:])
    out = []
    for k in range(GROUP // 2):
        source = (member - step * (core * (GROUP // 2) + k)) % GROUP
        own = lax.dynamic_index_in_dim(blocks, source, axis=2, keepdims=False)
        for g in range(groups):
            at = (group + g) % groups
            pair = lax.dynamic_index_in_dim(own, at, axis=1, keepdims=False)
            out.append(jnp.where(half == 0, pair, pair[::-1]))
    out = jnp.pad(jnp.stack(out), ((0, 0), (0, 0), (0, width - capacity), (0, 0), (0, 0)))
    return out.reshape(-1, *saved.shape[1:])


def shards(
    tokens_fwd,
    routes_fwd,
    gates_fwd,
    cotangent,
    routes_bwd,
    gates_bwd,
    saved_pre,
    w_gate,
    w_up,
    w_down,
):
    groups = lax.axis_size("group")
    devices = 2 * groups * GROUP
    capacity = saved_pre.shape[1] // devices
    width = -(-capacity // PAD) * PAD
    columns = tokens_fwd.shape[2]
    hidden_width = w_gate.shape[2]

    together = lax.optimization_barrier
    place_fwd = placing_of(routes_fwd[0, :, 0], capacity, width)
    place_bwd = placing_of(routes_bwd[0, :, 0], capacity, width)
    send_fwd = jnp.dot(place_fwd, tokens_fwd[0], preferred_element_type=F32).astype(BF16)
    scaled = (cotangent[0].astype(F32) * gates_bwd[0]).astype(BF16)
    send_bwd = jnp.dot(place_bwd, scaled, preferred_element_type=F32).astype(BF16)

    def flat(blocks):
        return blocks.reshape(-1, columns)

    fwd = widen(send_fwd.reshape(2, groups, width, columns))
    fwd, bwd = together((shift_groups(fwd), widen(send_bwd.reshape(2, groups, width, columns))))
    got_fwd = [flat(jnp.stack(fwd))]

    sections = lax.axis_size("section")
    up = [(i, i + 1) for i in range(sections - 1)]
    down = [(i + 1, i) for i in range(sections - 1)]
    send_up = jnp.stack([routes_fwd[0, :, 0].astype(F32), gates_fwd[0, :, 0]])
    send_down = routes_bwd[0, :, 0].astype(F32)
    bwd, send_up, send_down = together((bwd, send_up, send_down))
    from_before = lax.ppermute(send_up, "section", up)
    from_after = lax.ppermute(send_down, "section", down)

    part, bwd = together((around(got_fwd[0], 1), shift_groups(bwd)))
    got_fwd.append(part)
    got_bwd = [flat(jnp.stack(bwd))]
    for _ in range(2, GROUP):
        part, bwd = together((around(got_fwd[-1], 1), around(got_bwd[-1], -1)))
        got_fwd.append(part)
        got_bwd.append(bwd)
    last_bwd = around(got_bwd[-1], -1)

    partial_fwd = [
        jnp.concatenate(
            [
                jnp.dot(rows, w_gate[0], preferred_element_type=F32),
                jnp.dot(rows, w_up[0], preferred_element_type=F32),
            ],
            axis=1,
        )
        for rows in got_fwd
    ]
    summed = reduce_rows(partial_fwd)
    gate_pre, up_pre = jnp.split(summed, 2, axis=1)
    hidden = gather_rows((gate_pre * jax.nn.sigmoid(gate_pre) * up_pre).astype(BF16))
    hidden, last_bwd, from_before, from_after = together(
        (hidden, last_bwd, from_before, from_after)
    )
    got_bwd.append(last_bwd)
    out = [jnp.dot(rows, w_down[0], preferred_element_type=F32).astype(BF16) for rows in hidden]

    grad_hidden = reduce_rows([contract_last(rows, w_down[0]) for rows in got_bwd])
    saved = saved_half(saved_pre[0], capacity, width, -1)
    pre_gate = saved[:, 0].astype(F32)
    pre_up = saved[:, 1].astype(F32)
    sigmoid_gate = jax.nn.sigmoid(pre_gate)
    grad_gate = grad_hidden * pre_up * sigmoid_gate * (1.0 + pre_gate * (1.0 - sigmoid_gate))
    grad_up = grad_hidden * pre_gate * sigmoid_gate
    grads = gather_rows(jnp.concatenate([grad_gate, grad_up], axis=1).astype(BF16))
    total, grads = together((around(out[GROUP - 1], -1), grads))
    grad_out = [
        (
            contract_last(rows[:, :hidden_width], w_gate[0])
            + contract_last(rows[:, hidden_width:], w_up[0])
        ).astype(BF16)
        for rows in grads
    ]

    total_bwd = grad_out[GROUP - 1]
    for k in range(GROUP - 2, 0, -1):
        total, total_bwd = together((around(total + out[k], -1), around(total_bwd, 1)))
        total_bwd = total_bwd + grad_out[k]

    def blocks_of(rows):
        return rows.reshape(groups, 2 * width, columns)

    total, total_bwd = together((shift_groups(blocks_of(total + out[0])), around(total_bwd, 1)))

    def shifted(values, shift):
        mine, others = values[:, :width], values[:, width:]
        across = [(2 * i + h, 2 * j + 1 - h) for i, j in shift for h in range(2)]
        mine = lax.ppermute(mine, "section", shift)
        others = lax.ppermute(others, ("section", "half"), across)
        return flat(mine), flat(others)

    moved, total_bwd = together(
        (shifted(jnp.stack(total), up), shift_groups(blocks_of(total_bwd + grad_out[0])))
    )

    def rows_of(placing, values):
        mine, others = values
        cut = mine.shape[0]
        return lax.dot_general(
            placing[:cut], mine, (((0,), (0,)), ((), ())), preferred_element_type=F32
        ) + lax.dot_general(
            placing[cut:], others, (((0,), (0,)), ((), ())), preferred_element_type=F32
        )

    place_before = placing_of(from_before[0].astype(jnp.int32), capacity, width)
    place_after = placing_of(from_after.astype(jnp.int32), capacity, width)
    forwarded = rows_of(place_before, moved) * from_before[1][:, None]
    returned = rows_of(place_after, shifted(jnp.stack(total_bwd), down))
    return (forwarded.astype(BF16)[None], returned.astype(BF16)[None])


def solution(mesh):
    sections, expert_devices, quarters = (mesh.shape[name] for name in ("section", "expert", "dp"))
    fine = Mesh(
        mesh.devices.reshape(sections, 2, expert_devices // 2 // GROUP, GROUP, 2, quarters // 2),
        ("section", "half", "group", "member", "far", "core"),
    )
    expert, dp = ("half", "group", "member"), ("far", "core")
    return jax.shard_map(
        shards,
        mesh=fine,
        in_specs=(
            P("section", expert, dp),
            P("section", expert, None),
            P("section", expert, None),
            P("section", expert, dp),
            P("section", expert, None),
            P("section", expert, None),
            P("section", None, None, expert),
            P("section", dp, expert),
            P("section", dp, expert),
            P("section", expert, dp),
        ),
        out_specs=(P("section", expert, dp), P("section", expert, dp)),
        check_vma=False,
    )
```

```python
import jax
import jax.numpy as jnp
from jax import lax
from jax.sharding import Mesh
from jax.sharding import PartitionSpec as P

GROUP = 4
PAD = 8
RING = ("group", "member")
BF16 = jnp.bfloat16
F32 = jnp.float32


def hop(values, step):
    count = lax.axis_size(RING)
    return lax.ppermute(values, RING, [(i, (i + step) % count) for i in range(count)])


def swap(values, axis):
    return lax.ppermute(values, axis, [(0, 1), (1, 0)])


def placing_of(routes, capacity, width):
    groups = lax.axis_size("group")
    half, group = lax.axis_index("half"), lax.axis_index("group")
    near = [half * groups + (group + k) % groups for k in range(groups)]
    far = [(1 - half) * groups + (group + k) % groups for k in range(groups)]
    ids = jnp.stack(near + far).astype(jnp.int32)
    member = (routes[None, :] == ids[:, None]).astype(jnp.int32)
    before = jnp.cumsum(member, axis=1) - member
    slot_ids = jnp.arange(width, dtype=jnp.int32)
    hit = (before[:, None, :] == slot_ids[None, :, None]) & (slot_ids < capacity)[None, :, None]
    placing = jnp.where(hit & (member[:, None, :] > 0), 1.0, 0.0).astype(BF16)
    return placing.reshape(-1, routes.shape[0])


def dispatch(slots):
    member = lax.axis_index("member")
    other = swap(slots[1], "half")
    blocks = jnp.concatenate([slots[0], other], axis=1)
    own = blocks[0]
    right = jnp.stack([blocks[0], blocks[1]])
    left = jnp.stack([blocks[0], blocks[2]])
    rights, lefts = {}, {}
    for step in range(1, 8):
        if step == 4:
            right, left = right[1], left[1]
        right, left = hop(right, 1), hop(left, -1)
        rights[step], lefts[step] = right, left
    out = [jnp.stack([own, lefts[4], rights[4]])]
    for s in range(1, GROUP):
        out.append(
            jnp.stack(
                [
                    jnp.where(member >= s, rights[s][0], lefts[4 - s][0]),
                    jnp.where(member >= s, lefts[4 - s][1], lefts[8 - s]),
                    jnp.where(member < s, rights[s][1], rights[s + 4]),
                ]
            )
        )
    return [part.reshape(-1, slots.shape[-1]) for part in out]


def collect(parts):
    member = lax.axis_index("member")

    def only(mask, values):
        return jnp.where(mask, values, jnp.zeros_like(values))

    def back(right, left):
        return lax.optimization_barrier((hop(right, -1), hop(left, 1)))

    right, left = only(member >= 3, parts[3][2]), only(member < 1, parts[1][1])
    for s in (2, 1):
        right, left = back(right, left)
        right = right + only(member >= s, parts[s][2])
        left = left + only(member < GROUP - s, parts[GROUP - s][1])
    right, left = back(right, left)
    right, left = back(right + parts[0][2], left + parts[0][1])
    right = jnp.stack([only(member >= 3, parts[3][0]), right + only(member < 3, parts[3][2])])
    left = jnp.stack([only(member < 1, parts[1][0]), left + only(member >= 1, parts[1][1])])
    for s in (2, 1):
        t = GROUP - s
        right, left = back(right, left)
        right = right + jnp.stack(
            [only(member >= s, parts[s][0]), only(member < s, parts[s][2])]
        )
        left = left + jnp.stack([only(member < t, parts[t][0]), only(member >= t, parts[t][1])])
    right, left = back(right, left)
    return jnp.stack([parts[0][0] + right[0] + left[0], right[1], left[1]])


def reduce_rows(parts):
    place = lax.axis_index("core")
    low = jnp.concatenate(parts[: GROUP // 2])
    high = jnp.concatenate(parts[GROUP // 2 :])
    kept, sent = jnp.where(place == 0, low, high), jnp.where(place == 0, high, low)
    kept = kept + swap(sent, "core")
    return kept + swap(kept.astype(BF16), "far").astype(F32)


def gather_rows(values):
    place = lax.axis_index("core")
    other = swap(values, "core")
    low, high = jnp.where(place == 0, values, other), jnp.where(place == 0, other, values)
    rows = values.shape[0] // 2
    return [low[:rows], low[rows:], high[:rows], high[rows:]]


def contract_last(left_side, right_side):
    return lax.dot_general(
        left_side, right_side, (((1,), (1,)), ((), ())), preferred_element_type=F32
    )


def saved_half(saved, capacity, width, step):
    groups = lax.axis_size("group")
    half, group, member, core = (lax.axis_index(n) for n in ("half", "group", "member", "core"))
    blocks = saved.reshape(2, groups, GROUP, capacity, *saved.shape[1:])
    out = []
    for k in range(GROUP // 2):
        source = (member - step * (core * (GROUP // 2) + k)) % GROUP
        own = lax.dynamic_index_in_dim(blocks, source, axis=2, keepdims=False)
        for g in range(groups):
            at = (group + g) % groups
            pair = lax.dynamic_index_in_dim(own, at, axis=1, keepdims=False)
            out.append(jnp.where(half == 0, pair, pair[::-1]))
    out = jnp.pad(jnp.stack(out), ((0, 0), (0, 0), (0, width - capacity), (0, 0), (0, 0)))
    return out.reshape(-1, *saved.shape[1:])


def shards(
    tokens_fwd,
    routes_fwd,
    gates_fwd,
    cotangent,
    routes_bwd,
    gates_bwd,
    saved_pre,
    w_gate,
    w_up,
    w_down,
):
    groups = lax.axis_size("group")
    devices = 2 * groups * GROUP
    capacity = saved_pre.shape[1] // devices
    width = -(-capacity // PAD) * PAD
    columns = tokens_fwd.shape[2]
    hidden_width = w_gate.shape[2]

    place_fwd = placing_of(routes_fwd[0, :, 0], capacity, width)
    place_bwd = placing_of(routes_bwd[0, :, 0], capacity, width)
    send_fwd = jnp.dot(place_fwd, tokens_fwd[0], preferred_element_type=F32).astype(BF16)
    scaled = (cotangent[0].astype(F32) * gates_bwd[0]).astype(BF16)
    send_bwd = jnp.dot(place_bwd, scaled, preferred_element_type=F32).astype(BF16)

    got_fwd = dispatch(send_fwd.reshape(2, groups, width, columns))
    got_bwd = dispatch(send_bwd.reshape(2, groups, width, columns))

    sections = lax.axis_size("section")
    up = [(i, i + 1) for i in range(sections - 1)]
    down = [(i + 1, i) for i in range(sections - 1)]
    send_up = jnp.stack([routes_fwd[0, :, 0].astype(F32), gates_fwd[0, :, 0]])
    send_down = routes_bwd[0, :, 0].astype(F32)
    got_fwd, send_up, send_down = lax.optimization_barrier((got_fwd, send_up, send_down))
    from_before = lax.ppermute(send_up, "section", up)
    from_after = lax.ppermute(send_down, "section", down)

    partial_fwd = [
        jnp.concatenate(
            [
                jnp.dot(rows, w_gate[0], preferred_element_type=F32),
                jnp.dot(rows, w_up[0], preferred_element_type=F32),
            ],
            axis=1,
        )
        for rows in got_fwd
    ]
    summed = reduce_rows(partial_fwd)
    gate_pre, up_pre = jnp.split(summed, 2, axis=1)
    hidden = gather_rows((gate_pre * jax.nn.sigmoid(gate_pre) * up_pre).astype(BF16))
    out = [jnp.dot(rows, w_down[0], preferred_element_type=F32).astype(BF16) for rows in hidden]

    grad_hidden = reduce_rows([contract_last(rows, w_down[0]) for rows in got_bwd])
    saved = saved_half(saved_pre[0], capacity, width, 1)
    pre_gate = saved[:, 0].astype(F32)
    pre_up = saved[:, 1].astype(F32)
    sigmoid_gate = jax.nn.sigmoid(pre_gate)
    grad_gate = grad_hidden * pre_up * sigmoid_gate * (1.0 + pre_gate * (1.0 - sigmoid_gate))
    grad_up = grad_hidden * pre_gate * sigmoid_gate
    grads = gather_rows(jnp.concatenate([grad_gate, grad_up], axis=1).astype(BF16))
    grad_out = [
        (
            contract_last(rows[:, :hidden_width], w_gate[0])
            + contract_last(rows[:, hidden_width:], w_up[0])
        ).astype(BF16)
        for rows in grads
    ]

    def collected(parts):
        return collect([rows.reshape(groups, 2 * width, columns) for rows in parts])

    back_fwd, from_before = lax.optimization_barrier((collected(out), from_before))
    back_bwd, from_after = lax.optimization_barrier((collected(grad_out), from_after))

    def shifted(values, shift):
        mine, others = values[:, :width], values[:, width:]
        across = [(2 * i + h, 2 * j + 1 - h) for i, j in shift for h in range(2)]
        mine = lax.ppermute(mine, "section", shift)
        others = lax.ppermute(others, ("section", "half"), across)
        return mine.reshape(-1, columns), others.reshape(-1, columns)

    def rows_of(placing, values):
        mine, others = values
        cut = mine.shape[0]
        return lax.dot_general(
            placing[:cut], mine, (((0,), (0,)), ((), ())), preferred_element_type=F32
        ) + lax.dot_general(
            placing[cut:], others, (((0,), (0,)), ((), ())), preferred_element_type=F32
        )

    place_before = placing_of(from_before[0].astype(jnp.int32), capacity, width)
    place_after = placing_of(from_after.astype(jnp.int32), capacity, width)
    forwarded = rows_of(place_before, shifted(back_fwd, up)) * from_before[1][:, None]
    returned = rows_of(place_after, shifted(back_bwd, down))
    return (forwarded.astype(BF16)[None], returned.astype(BF16)[None])


def solution(mesh):
    sections, expert_devices, quarters = (mesh.shape[name] for name in ("section", "expert", "dp"))
    fine = Mesh(
        mesh.devices.reshape(sections, 2, expert_devices // 2 // GROUP, GROUP, 2, quarters // 2),
        ("section", "half", "group", "member", "far", "core"),
    )
    expert, dp = ("half", "group", "member"), ("far", "core")
    return jax.shard_map(
        shards,
        mesh=fine,
        in_specs=(
            P("section", expert, dp),
            P("section", expert, None),
            P("section", expert, None),
            P("section", expert, dp),
            P("section", expert, None),
            P("section", expert, None),
            P("section", None, None, expert),
            P("section", dp, expert),
            P("section", dp, expert),
            P("section", expert, dp),
        ),
        out_specs=(P("section", expert, dp), P("section", expert, dp)),
        check_vma=False,
    )
```

```python
import jax
import jax.numpy as jnp
from jax import lax
from jax.sharding import Mesh
from jax.sharding import PartitionSpec as P

GROUP = 4
PAD = 8
RING = ("group", "member")
BF16 = jnp.bfloat16
F32 = jnp.float32


def hop(values, step):
    count = lax.axis_size(RING)
    return lax.ppermute(values, RING, [(i, (i + step) % count) for i in range(count)])


def swap(values, axis):
    return lax.ppermute(values, axis, [(0, 1), (1, 0)])


def placing_of(routes, capacity, width):
    groups = lax.axis_size("group")
    half, group = lax.axis_index("half"), lax.axis_index("group")
    near = [half * groups + (group + k) % groups for k in range(groups)]
    far = [(1 - half) * groups + (group + k) % groups for k in range(groups)]
    ids = jnp.stack(near + far).astype(jnp.int32)
    member = (routes[None, :] == ids[:, None]).astype(jnp.int32)
    before = jnp.cumsum(member, axis=1) - member
    slot_ids = jnp.arange(width, dtype=jnp.int32)
    hit = (before[:, None, :] == slot_ids[None, :, None]) & (slot_ids < capacity)[None, :, None]
    placing = jnp.where(hit & (member[:, None, :] > 0), 1.0, 0.0).astype(BF16)
    return placing.reshape(-1, routes.shape[0])


def around(values, step):
    return lax.ppermute(values, "member", [(i, (i + step) % GROUP) for i in range(GROUP)])


def dispatch(slots, step):
    blocks = jnp.concatenate([slots[0], swap(slots[1], "half")], axis=1)
    part = jnp.stack([blocks[0], hop(blocks[2], -GROUP), hop(blocks[1], GROUP)])
    part = part.reshape(-1, slots.shape[-1])
    parts = [part]
    for _ in range(1, GROUP):
        part = around(part, step)
        parts.append(part)
    return parts


def collect(parts, step, groups):
    total = parts[GROUP - 1]
    for k in range(GROUP - 2, -1, -1):
        total = around(total, -step) + parts[k]
    total = total.reshape(groups, 2, -1, total.shape[-1])
    blocks = jnp.stack([total[0], hop(total[2], -GROUP), hop(total[1], GROUP)])
    return blocks[:, 0], blocks[:, 1]


def reduce_rows(parts):
    place = lax.axis_index("core")
    low = jnp.concatenate(parts[: GROUP // 2])
    high = jnp.concatenate(parts[GROUP // 2 :])
    kept, sent = jnp.where(place == 0, low, high), jnp.where(place == 0, high, low)
    kept = kept + swap(sent, "core")
    return kept + swap(kept.astype(BF16), "far").astype(F32)


def gather_rows(values):
    place = lax.axis_index("core")
    other = swap(values, "core")
    low, high = jnp.where(place == 0, values, other), jnp.where(place == 0, other, values)
    rows = values.shape[0] // 2
    return [low[:rows], low[rows:], high[:rows], high[rows:]]


def contract_last(left_side, right_side):
    return lax.dot_general(
        left_side, right_side, (((1,), (1,)), ((), ())), preferred_element_type=F32
    )


def saved_half(saved, capacity, width, step):
    groups = lax.axis_size("group")
    half, group, member, core = (lax.axis_index(n) for n in ("half", "group", "member", "core"))
    blocks = saved.reshape(2, groups, GROUP, capacity, *saved.shape[1:])
    out = []
    for k in range(GROUP // 2):
        source = (member - step * (core * (GROUP // 2) + k)) % GROUP
        own = lax.dynamic_index_in_dim(blocks, source, axis=2, keepdims=False)
        for g in range(groups):
            at = (group + g) % groups
            pair = lax.dynamic_index_in_dim(own, at, axis=1, keepdims=False)
            out.append(jnp.where(half == 0, pair, pair[::-1]))
    out = jnp.pad(jnp.stack(out), ((0, 0), (0, 0), (0, width - capacity), (0, 0), (0, 0)))
    return out.reshape(-1, *saved.shape[1:])


def shards(
    tokens_fwd,
    routes_fwd,
    gates_fwd,
    cotangent,
    routes_bwd,
    gates_bwd,
    saved_pre,
    w_gate,
    w_up,
    w_down,
):
    groups = lax.axis_size("group")
    devices = 2 * groups * GROUP
    capacity = saved_pre.shape[1] // devices
    width = -(-capacity // PAD) * PAD
    columns = tokens_fwd.shape[2]
    hidden_width = w_gate.shape[2]

    place_fwd = placing_of(routes_fwd[0, :, 0], capacity, width)
    place_bwd = placing_of(routes_bwd[0, :, 0], capacity, width)
    send_fwd = jnp.dot(place_fwd, tokens_fwd[0], preferred_element_type=F32).astype(BF16)
    scaled = (cotangent[0].astype(F32) * gates_bwd[0]).astype(BF16)
    send_bwd = jnp.dot(place_bwd, scaled, preferred_element_type=F32).astype(BF16)

    got_fwd = dispatch(send_fwd.reshape(2, groups, width, columns), 1)
    got_bwd = dispatch(send_bwd.reshape(2, groups, width, columns), -1)

    sections = lax.axis_size("section")
    up = [(i, i + 1) for i in range(sections - 1)]
    down = [(i + 1, i) for i in range(sections - 1)]
    send_up = jnp.stack([routes_fwd[0, :, 0].astype(F32), gates_fwd[0, :, 0]])
    send_down = routes_bwd[0, :, 0].astype(F32)
    got_fwd[1], send_up, send_down = lax.optimization_barrier((got_fwd[1], send_up, send_down))
    from_before = lax.ppermute(send_up, "section", up)
    from_after = lax.ppermute(send_down, "section", down)
    got_fwd[3], from_before, from_after = lax.optimization_barrier(
        (got_fwd[3], from_before, from_after)
    )

    partial_fwd = [
        jnp.concatenate(
            [
                jnp.dot(rows, w_gate[0], preferred_element_type=F32),
                jnp.dot(rows, w_up[0], preferred_element_type=F32),
            ],
            axis=1,
        )
        for rows in got_fwd
    ]
    summed = reduce_rows(partial_fwd)
    gate_pre, up_pre = summed[:, :hidden_width], summed[:, hidden_width:]
    hidden = gather_rows((gate_pre * jax.nn.sigmoid(gate_pre) * up_pre).astype(BF16))
    out = [jnp.dot(rows, w_down[0], preferred_element_type=F32).astype(BF16) for rows in hidden]
    back_fwd = collect(out, 1, groups)

    grad_hidden = reduce_rows([contract_last(rows, w_down[0]) for rows in got_bwd])
    saved = saved_half(saved_pre[0], capacity, width, -1)
    pre_gate = saved[:, 0].astype(F32)
    pre_up = saved[:, 1].astype(F32)
    sigmoid_gate = jax.nn.sigmoid(pre_gate)
    grad_gate = grad_hidden * pre_up * sigmoid_gate * (1.0 + pre_gate * (1.0 - sigmoid_gate))
    grad_up = grad_hidden * pre_gate * sigmoid_gate
    grads = gather_rows(jnp.concatenate([grad_gate, grad_up], axis=1).astype(BF16))
    grad_out = [
        (
            contract_last(rows[:, :hidden_width], w_gate[0])
            + contract_last(rows[:, hidden_width:], w_up[0])
        ).astype(BF16)
        for rows in grads
    ]
    back_bwd = collect(grad_out, -1, groups)

    def shifted(values, shift):
        across = [(2 * i + h, 2 * j + 1 - h) for i, j in shift for h in range(2)]
        mine = lax.ppermute(values[0], "section", shift)
        others = lax.ppermute(values[1], ("section", "half"), across)
        return mine.reshape(-1, columns), others.reshape(-1, columns)

    def rows_of(placing, values):
        mine, others = values
        cut = mine.shape[0]
        return lax.dot_general(
            placing[:cut], mine, (((0,), (0,)), ((), ())), preferred_element_type=F32
        ) + lax.dot_general(
            placing[cut:], others, (((0,), (0,)), ((), ())), preferred_element_type=F32
        )

    place_before = placing_of(from_before[0].astype(jnp.int32), capacity, width)
    place_after = placing_of(from_after.astype(jnp.int32), capacity, width)
    forwarded = rows_of(place_before, shifted(back_fwd, up)) * from_before[1][:, None]
    returned = rows_of(place_after, shifted(back_bwd, down))
    return (forwarded.astype(BF16)[None], returned.astype(BF16)[None])


def solution(mesh):
    sections, expert_devices, quarters = (mesh.shape[name] for name in ("section", "expert", "dp"))
    fine = Mesh(
        mesh.devices.reshape(sections, 2, expert_devices // 2 // GROUP, GROUP, 2, quarters // 2),
        ("section", "half", "group", "member", "far", "core"),
    )
    expert, dp = ("half", "group", "member"), ("far", "core")
    return jax.shard_map(
        shards,
        mesh=fine,
        in_specs=(
            P("section", expert, dp),
            P("section", expert, None),
            P("section", expert, None),
            P("section", expert, dp),
            P("section", expert, None),
            P("section", expert, None),
            P("section", None, None, expert),
            P("section", dp, expert),
            P("section", dp, expert),
            P("section", expert, dp),
        ),
        out_specs=(P("section", expert, dp), P("section", expert, dp)),
        check_vma=False,
    )
```
